512 devices in a mesh: gx: 8 (over x, z_hi), gy: 8 (over y, core), gz: 8 (over z_lo).
Axes of the slice: x: 4, y: 4, z: 16 (z_hi: 2, z_lo: 8; z = z_hi * 8 + z_lo), core: 2. Of those that a mesh axis runs over, the one named last changes fastest.
Arguments:
- tokens: bfloat16 [1024, 8192], P('gx', ('gz', 'gy')), may hold values from -6 to 6
- cotangent: bfloat16 [1024, 8192], P('gx', ('gz', 'gy')), may hold values from -6 to 6
- gate_weight: bfloat16 [8192, 14336], P(('gz', 'gx'), 'gy'), may hold values from -0.0625 to 0.0625
- up_weight: bfloat16 [8192, 14336], P(('gz', 'gx'), 'gy'), may hold values from -0.0625 to 0.0625
- down_weight: bfloat16 [14336, 8192], P('gy', ('gz', 'gx')), may hold values from -0.046875 to 0.046875
Outputs:
- output: bfloat16 [1024, 8192], P('gx', ('gz', 'gy'))
- input_grad: bfloat16 [1024, 8192], P('gx', ('gz', 'gy'))
- gate_grad: bfloat16 [8192, 14336], P('gz', ('gy', 'gx'))
- up_grad: bfloat16 [8192, 14336], P('gz', ('gy', 'gx'))
- down_grad: bfloat16 [14336, 8192], P(('gy', 'gx'), 'gz')
The draws below stay inside these ranges and needn't reach their ends.
All inputs are finite; a program needn't handle non-finite values.
Results may differ from the reference program's by a relative error of at most 0.0049.
Values may be sent and summed in bfloat16 or wider, within the bound.
No kernel may reach another device: no remote copies, remote signals or barrier semaphores. Data moves between devices by JAX's collectives and lax.ppermute only.
A program may use at most 64 MiB of HBM per device.

```python
import jax
import jax.numpy as jnp
from jax import lax

D = 8192
FF = 14336
TOKENS = 1024


def level_of(own_key, extent, cuts, smallest, largest):
    def one(dim, blocks):
        draws = jax.random.uniform(jax.random.fold_in(jax.random.fold_in(own_key, 6), dim), (blocks,), jnp.float32, smallest / len(cuts), largest / len(cuts))
        return jnp.repeat(jnp.exp(draws), extent[dim] // blocks).reshape((-1,) + (1,) * (len(extent) - dim - 1))

    level = one(*cuts[0])
    for cut in cuts[1:]:
        level = level * one(*cut)
    return level


def gaussian(key, dims, deviation, bound, split=(), held_as=jnp.bfloat16):
    values = jax.random.normal(key, dims, jnp.float32) * deviation
    if len(split) > 0:
        values = level_of(key, dims, split, -0.22, 0.18) * values
    return jnp.clip(values, min=-bound, max=bound).astype(held_as)


def setup_inputs(seed: int = 0) -> dict:
    key_of = jax.random.split(jax.random.key(seed), 6)
    return {
        "tokens": gaussian(key_of[0], (TOKENS, D), 1.0, 6.0, ((0, 8), (1, 64))),
        "cotangent": gaussian(key_of[1], (TOKENS, D), 1.0, 6.0, ((0, 8), (1, 64))),
        "gate_weight": gaussian(key_of[2], (D, FF), D ** -0.5, 0.0625, ((0, 64), (1, 8))),
        "up_weight": gaussian(key_of[3], (D, FF), D ** -0.5, 0.0625, ((0, 64), (1, 8))),
        "down_weight": gaussian(key_of[4], (FF, D), FF ** -0.5, 0.046875, ((0, 8), (1, 64))),
    }


def contract_rows(left, right):
    return lax.dot_general(left, right, (((0,), (0,)), ((), ())), preferred_element_type=jnp.float32)


def contract_cols(left, right):
    return lax.dot_general(left, right, (((1,), (1,)), ((), ())), preferred_element_type=jnp.float32)


def reference(tokens, cotangent, gate_weight, up_weight, down_weight):
    gate = jnp.dot(tokens, gate_weight, preferred_element_type=jnp.float32)
    upper = jnp.dot(tokens, up_weight, preferred_element_type=jnp.float32)
    sigma = jax.nn.sigmoid(gate)
    activated = gate * sigma
    hidden = (activated * upper).astype(jnp.bfloat16)
    output = jnp.dot(hidden, down_weight, preferred_element_type=jnp.float32).astype(jnp.bfloat16)
    hidden_grad = contract_cols(cotangent, down_weight)
    gate_delta = (hidden_grad * upper * sigma * (1.0 + gate * (1.0 - sigma))).astype(jnp.bfloat16)
    up_delta = (hidden_grad * activated).astype(jnp.bfloat16)
    input_grad = (contract_cols(gate_delta, gate_weight) + contract_cols(up_delta, up_weight)).astype(jnp.bfloat16)
    down_grad = contract_rows(hidden, cotangent).astype(jnp.bfloat16)
    gate_grad = contract_rows(tokens, gate_delta).astype(jnp.bfloat16)
    up_grad = contract_rows(tokens, up_delta).astype(jnp.bfloat16)
    return (output, input_grad, gate_grad, up_grad, down_grad)
```

```python
import jax
import jax.numpy as jnp
from jax import lax
from jax.sharding import Mesh, PartitionSpec as P

BF = jnp.bfloat16
F32 = jnp.float32
WIRE = jnp.bfloat16
DEPTH = ("zh", "gz")


def dot(left, right, left_dim, right_dim):
    return lax.dot_general(
        left, right, (((left_dim,), (right_dim,)), ((), ())), preferred_element_type=F32
    )


def swap(value, axis):
    return lax.ppermute(value, axis, [(0, 1), (1, 0)])


def shift(value, by):
    return lax.ppermute(value, DEPTH, [(i, (i + by) % 16) for i in range(16)])


def ordered(own, other, index):
    first = index == 0
    return jnp.stack([jnp.where(first, own, other), jnp.where(first, other, own)])


def take(value, index, dim=0):
    return lax.dynamic_index_in_dim(value, index, dim, keepdims=False)


def gather_plane(both):
    core = lax.axis_index("c")
    both = jnp.broadcast_to(both[None], (16,) + both.shape)
    own = lax.all_to_all(both, ("x", "y"), 0, 0, tiled=True)
    own = own.reshape((4, 4) + own.shape[1:])
    pair = ordered(own, swap(own, "c"), core)
    return pair.transpose(3, 1, 0, 4, 2, 5)


def per_device(tokens, cotangent, gate_weight, up_weight, down_weight):
    zh, core = lax.axis_index("zh"), lax.axis_index("c")
    level = lax.axis_index(DEPTH)
    tok, feat = tokens.shape
    cols = gate_weight.shape[1] // 4

    both = jnp.stack([tokens, cotangent])
    near = lax.ppermute(both, ("zh", "c"), [(0, 0), (1, 2), (2, 1), (3, 3)])
    far = lax.ppermute(both, ("zh", "c"), [(0, 2), (1, 0), (2, 3), (3, 1)])

    gate_up = jnp.concatenate(
        [gate_weight.reshape(tok, 4, cols), up_weight.reshape(tok, 4, cols)], axis=2
    )
    gate_up = lax.all_to_all(gate_up, "x", 1, 0).reshape(4 * tok, 2 * cols)
    down = lax.all_to_all(down_weight, "x", 0, 1, tiled=True)

    near = gather_plane(near)
    far = gather_plane(far)
    whole = ordered(near, far, zh)
    whole = whole.transpose(1, 2, 3, 4, 5, 0, 6).reshape(2, 8 * tok, 8 * feat)

    blocks = near.reshape(2, 4, 4, tok // 2, 4 * feat)

    def partial(by):
        rows = take(blocks, lax.rem(level + by + 16, 4), 2).reshape(2, 2 * tok, 4 * feat)
        return jnp.concatenate(
            [dot(rows[0], gate_up, 1, 0), dot(rows[1], down, 1, 1)], axis=1
        ).reshape(4, tok // 2, 3 * cols)

    across = partial(2).astype(WIRE)
    upward = shift(across[:2], 2)
    downward = shift(across[2:], -2)
    after = shift(partial(1).astype(WIRE), 1)
    before = shift(partial(-1).astype(WIRE), -1)
    part = partial(0)
    part = part + after.astype(F32) + before.astype(F32)
    part = part + jnp.concatenate([upward, downward]).astype(F32)
    row = level // 4

    def owed(by):
        return shift(take(part, lax.rem(row + by + 4, 4)).astype(WIRE), 4 * by)

    total = owed(2).astype(F32) + owed(1).astype(F32) + owed(-1).astype(F32)
    total = total + take(part, row)

    gate, upper, hidden_grad = (total[:, i * cols : (i + 1) * cols] for i in range(3))
    sigma = jax.nn.sigmoid(gate)
    activated = gate * sigma
    hidden = (activated * upper).astype(BF)
    gate_delta = (hidden_grad * upper * sigma * (1.0 + gate * (1.0 - sigma))).astype(BF)
    up_delta = (hidden_grad * activated).astype(BF)
    mine = jnp.concatenate([gate_delta, up_delta, hidden], axis=1)

    quarter = jnp.zeros((4,) + mine.shape, BF)
    quarter = lax.dynamic_update_index_in_dim(quarter, mine, row, 0)
    for by in (2, 1, -1):
        quarter = lax.dynamic_update_index_in_dim(
            quarter, shift(mine, 4 * by), lax.rem(row - by + 4, 4), 0
        )
    all_of = jnp.zeros((4,) + quarter.shape, BF)

    def put(buffer, value, by, start=0):
        at = lax.rem(level - by + 16, 4)
        return lax.dynamic_update_slice(buffer, value[:, None], (start, at, 0, 0))

    all_of = put(all_of, quarter, 0)
    all_of = put(all_of, shift(quarter, 1), 1)
    all_of = put(all_of, shift(quarter, -1), -1)
    all_of = put(all_of, shift(quarter[:2], 2), 2)
    all_of = put(all_of, shift(quarter[2:], -2), 2, 2)

    by_zh = all_of.reshape(4, 2, tok, 3 * cols)

    def parts(which):
        rows = take(by_zh, which, 1).reshape(4 * tok, 3 * cols)
        return jnp.stack(
            [dot(rows[:, 2 * cols :], down, 1, 0), dot(rows[:, : 2 * cols], gate_up, 1, 1)]
        )

    got = swap(parts(1 - core), "c")
    sums = (parts(core) + got).astype(BF)
    sums = sums.reshape(2, 4, tok, 4, feat).transpose(1, 3, 0, 2, 4)
    sums = lax.all_to_all(
        sums.reshape(16, 2, tok, feat), ("x", "y"), 0, 0, tiled=True
    )
    result = jnp.sum(sums.astype(F32), axis=0).astype(BF)
    result = lax.ppermute(result, ("zh", "c"), [(0, 0), (1, 2), (2, 1), (3, 3)])

    every = all_of.reshape(8 * tok, 3 * cols)
    half = cols // 2

    def own_half(at):
        return jnp.where(
            zh == 0, every[:, at : at + half], every[:, at + half : at + cols]
        )

    gate_grad = dot(whole[0], own_half(0), 0, 0)
    up_grad = dot(whole[0], own_half(cols), 0, 0)
    down_grad = dot(own_half(2 * cols), whole[1], 0, 0)
    return (
        result[0],
        result[1],
        gate_grad.astype(BF),
        up_grad.astype(BF),
        down_grad.astype(BF),
    )


def solution(mesh):
    fine = Mesh(mesh.devices.reshape(4, 2, 4, 2, 8), ("x", "zh", "y", "c", "gz"))
    gx, gy = ("x", "zh"), ("y", "c")
    act = P(gx, ("gz",) + gy)
    return jax.shard_map(
        per_device,
        mesh=fine,
        in_specs=(act, act, P(("gz",) + gx, gy), P(("gz",) + gx, gy), P(gy, ("gz",) + gx)),
        out_specs=(act, act, P("gz", gy + gx), P("gz", gy + gx), P(gy + gx, "gz")),
        check_vma=False,
    )
```

```python
import jax
import jax.numpy as jnp
from jax import lax
from jax.experimental import pallas as pl
from jax.experimental.pallas import tpu as pltpu
from jax.sharding import Mesh, PartitionSpec as P

BF = jnp.bfloat16
F32 = jnp.float32
DEPTH = ("zh", "gz")
TURN = [(0, 0), (1, 2), (2, 1), (3, 3)]


def dot(left, right, left_dim, right_dim):
    return lax.dot_general(
        left, right, (((left_dim,), (right_dim,)), ((), ())), preferred_element_type=F32
    )


def swap(value, axis):
    return lax.ppermute(value, axis, [(0, 1), (1, 0)])


def take(value, index, dim=0):
    return lax.dynamic_index_in_dim(value, index, dim, keepdims=False)


def tokens_of(ref, array, ys):
    return jnp.concatenate(
        [jnp.concatenate([ref[x, y, array] for x in range(4)], axis=0) for y in ys],
        axis=1,
    )


def partial_kernel(core_ref, own_ref, other_ref, weight_ref, out_ref):
    cols = weight_ref.shape[2] // 3
    tok = own_ref.shape[3]
    weight = weight_ref[...].reshape(-1, 3 * cols)

    def work(ref, k):
        pair = dot(tokens_of(ref, 0, range(4)), weight[:, : 2 * cols], 1, 0)
        last = dot(tokens_of(ref, 1, range(4)), weight[:, 2 * cols :], 1, 0)
        out_ref[:, k, :, : 2 * cols] = pair.reshape(4, tok, 2 * cols)
        out_ref[:, k, :, 2 * cols :] = last.reshape(4, tok, cols)

    for core in range(2):

        @pl.when(core_ref[0] == core)
        def _():
            work(own_ref, core)
            work(other_ref, 1 - core)


def parts_kernel(which_ref, rows_ref, weight_ref, *rest):
    cols = weight_ref.shape[2] // 3
    rows = rows_ref[:, which_ref[0]].reshape(-1, 3 * cols)
    weight = weight_ref[...].reshape(-1, 3 * cols)
    output = dot(rows[:, 2 * cols :], weight[:, 2 * cols :], 1, 1)
    inner = dot(rows[:, : 2 * cols], weight[:, : 2 * cols], 1, 1)
    if len(rest) == 1:
        rest[0][0] = output
        rest[0][1] = inner
        return
    got_ref, out_ref = rest
    tok, feat = out_ref.shape[3:]
    for index, value in enumerate((output, inner)):
        value = (value + got_ref[index]).astype(BF)
        for x in range(4):
            for y in range(4):
                out_ref[x, y, index] = value[
                    x * tok : (x + 1) * tok, y * feat : (y + 1) * feat
                ]


def grads_kernel(place_ref, pieces_ref, rows_ref, gate_ref, up_ref, down_ref):
    part = gate_ref.shape[0]
    zh, core = place_ref[0], place_ref[1]
    width = 2 * pieces_ref.shape[6]
    for y in range(4):
        blocks = []
        for array in range(2):
            sides = []
            for parity in range(2):
                far = jnp.where(zh == parity, 0, 1)
                rows = []
                for x in range(4):
                    for k in range(2):
                        other = jnp.where(core == k, 0, 1)
                        rows.append(pieces_ref[far, other, x, y, array])
                sides.append(jnp.concatenate(rows, axis=0))
            blocks.append(jnp.concatenate(sides, axis=1))
        at = slice(y * width, (y + 1) * width)
        pair = dot(rows_ref[: 2 * part], blocks[0], 1, 0).astype(BF)
        gate_ref[:, at] = pair[:part]
        up_ref[:, at] = pair[part:]
        down_ref[:, at] = dot(rows_ref[2 * part :], blocks[1], 1, 0).astype(BF)


def local_call(kernel, shape, flops, scalars, *arrays):
    smem = pl.BlockSpec(memory_space=pltpu.SMEM)
    vmem = pl.BlockSpec(memory_space=pltpu.VMEM)
    return pl.pallas_call(
        kernel,
        out_shape=shape,
        in_specs=[smem] + [vmem] * len(arrays),
        out_specs=jax.tree.map(lambda _: vmem, shape),
        compiler_params=pltpu.CompilerParams(vmem_limit_bytes=40 * 2**20),
        cost_estimate=pl.CostEstimate(
            flops=flops, bytes_accessed=6 * 2**20, transcendentals=0
        ),
    )(scalars, *arrays)


def gather_plane(both):
    both = jnp.broadcast_to(both[None], (16,) + both.shape)
    own = lax.all_to_all(both, ("x", "y"), 0, 0, tiled=True)
    own = own.reshape((4, 4) + own.shape[1:])
    return own, swap(own, "c")


def per_device(tokens, cotangent, gate_weight, up_weight, down_weight):
    x, zh, core = (lax.axis_index(name) for name in ("x", "zh", "c"))
    tok, feat = tokens.shape
    cols = gate_weight.shape[1] // 4
    wide = 3 * cols
    flops = 2 * 8 * tok * 4 * feat * wide

    both = jnp.stack([tokens, cotangent])
    near = lax.ppermute(both, ("zh", "c"), TURN)

    mixed = jnp.concatenate(
        [
            gate_weight.reshape(tok, 4, cols),
            up_weight.reshape(tok, 4, cols),
            down_weight.T.reshape(tok, 4, cols),
        ],
        axis=2,
    ).transpose(1, 0, 2)
    weight = jnp.zeros_like(mixed)
    weight = lax.dynamic_update_index_in_dim(weight, take(mixed, x), x, 0)
    for by in (1, 2, 3):
        sent = lax.ppermute(
            take(mixed, lax.rem(x + by, 4)), "x", [(i, (i + by) % 4) for i in range(4)]
        )
        weight = lax.dynamic_update_index_in_dim(weight, sent, lax.rem(x + 4 - by, 4), 0)

    own, other = gather_plane(near)

    part = local_call(
        partial_kernel,
        jax.ShapeDtypeStruct((4, 2, tok, wide), F32),
        flops,
        jnp.stack([core]),
        own,
        other,
        weight,
    )
    both, part = lax.optimization_barrier((both, part))
    total = lax.psum_scatter(
        part.reshape(8 * tok, wide), DEPTH, scatter_dimension=0, tiled=True
    )

    far = lax.ppermute(both, ("zh", "c"), [(0, 2), (1, 0), (2, 3), (3, 1)])
    far_own, far_other = gather_plane(far)
    pieces = jnp.stack([own, other, far_own, far_other])
    pieces = pieces.reshape((2, 2) + own.shape)

    gate, upper, hidden_grad = (total[:, i * cols : (i + 1) * cols] for i in range(3))
    sigma = jax.nn.sigmoid(gate)
    activated = gate * sigma
    hidden = (activated * upper).astype(BF)
    gate_delta = (hidden_grad * upper * sigma * (1.0 + gate * (1.0 - sigma))).astype(BF)
    up_delta = (hidden_grad * activated).astype(BF)
    mine = jnp.concatenate([gate_delta, up_delta, hidden], axis=1)
    mine, pieces = lax.optimization_barrier((mine, pieces))
    every = lax.all_gather(mine, DEPTH, axis=0, tiled=True)

    by_zh = every.reshape(4, 2, tok, wide)
    give = local_call(
        parts_kernel,
        jax.ShapeDtypeStruct((2, 4 * tok, 4 * feat), F32),
        flops // 2,
        jnp.stack([1 - core]),
        by_zh,
        weight,
    )
    sums = local_call(
        parts_kernel,
        jax.ShapeDtypeStruct((4, 4, 2, tok, feat), BF),
        flops // 2,
        jnp.stack([core]),
        by_zh,
        weight,
        swap(give, "c"),
    )
    sums = lax.all_to_all(
        sums.reshape(16, 2, tok, feat), ("x", "y"), 0, 0, tiled=True
    )
    result = jnp.sum(sums.astype(F32), axis=0).astype(BF)
    result = lax.ppermute(result, ("zh", "c"), TURN)

    half = cols // 2

    def own_half(at):
        return jnp.where(
            zh == 0, every[:, at : at + half], every[:, at + half : at + cols]
        )

    rows = jnp.concatenate([own_half(i * cols) for i in range(3)], axis=1).T
    grad = jax.ShapeDtypeStruct((half, 8 * feat), BF)
    gate_grad, up_grad, down_grad = local_call(
        grads_kernel,
        (grad, grad, grad),
        flops,
        jnp.stack([zh, core]),
        pieces,
        rows,
    )
    return result[0], result[1], gate_grad.T, up_grad.T, down_grad


def solution(mesh):
    fine = Mesh(mesh.devices.reshape(4, 2, 4, 2, 8), ("x", "zh", "y", "c", "gz"))
    gx, gy = ("x", "zh"), ("y", "c")
    act = P(gx, ("gz",) + gy)
    return jax.shard_map(
        per_device,
        mesh=fine,
        in_specs=(act, act, P(("gz",) + gx, gy), P(("gz",) + gx, gy), P(gy, ("gz",) + gx)),
        out_specs=(act, act, P("gz", gy + gx), P("gz", gy + gx), P(gy + gx, "gz")),
        check_vma=False,
    )
```

```python
import functools

import jax
import jax.numpy as jnp
from jax import lax
from jax.experimental import pallas as pl
from jax.experimental.pallas import tpu as pltpu
from jax.sharding import Mesh, PartitionSpec as P

BF = jnp.bfloat16
F32 = jnp.float32
DEPTH = ("zh", "gz")
TURN = [(0, 0), (1, 2), (2, 1), (3, 3)]


def dot(left, right, left_dim, right_dim):
    return lax.dot_general(
        left, right, (((left_dim,), (right_dim,)), ((), ())), preferred_element_type=F32
    )


def swap(value, axis):
    return lax.ppermute(value, axis, [(0, 1), (1, 0)])


def shift(value, by):
    return lax.ppermute(value, DEPTH, [(i, (i + by) % 16) for i in range(16)])


def gather_depth(mine):
    level = lax.axis_index(DEPTH)
    row = level // 4
    quarter = jnp.zeros((4,) + mine.shape, BF)
    quarter = lax.dynamic_update_index_in_dim(quarter, mine, row, 0)
    for by in (2, 1, -1):
        quarter = lax.dynamic_update_index_in_dim(
            quarter, shift(mine, 4 * by), lax.rem(row - by + 4, 4), 0
        )
    every = jnp.zeros((4,) + quarter.shape, BF)
    pieces = (
        (quarter, 0, 0),
        (shift(quarter, 1), 1, 0),
        (shift(quarter, -1), -1, 0),
        (shift(quarter[:2], 2), 2, 0),
        (shift(quarter[2:], -2), 2, 2),
    )
    for value, by, start in pieces:
        at = lax.rem(level - by + 16, 4)
        every = lax.dynamic_update_slice(every, value[:, None], (start, at, 0, 0))
    return every.reshape(16 * mine.shape[0], mine.shape[1])


def take(value, index, dim=0):
    return lax.dynamic_index_in_dim(value, index, dim, keepdims=False)


def tokens_of(ref, array, ys):
    return jnp.concatenate(
        [jnp.concatenate([ref[x, y, array] for x in range(4)], axis=0) for y in ys],
        axis=1,
    )


def partial_kernel(core_ref, own_ref, other_ref, weight_ref, out_ref):
    cols = weight_ref.shape[2] // 3
    tok = own_ref.shape[3]
    weight = weight_ref[...].reshape(-1, 3 * cols)

    def work(ref, k):
        pair = dot(tokens_of(ref, 0, range(4)), weight[:, : 2 * cols], 1, 0)
        last = dot(tokens_of(ref, 1, range(4)), weight[:, 2 * cols :], 1, 0)
        out_ref[:, k, :, : 2 * cols] = pair.reshape(4, tok, 2 * cols)
        out_ref[:, k, :, 2 * cols :] = last.reshape(4, tok, cols)

    for core in range(2):

        @pl.when(core_ref[0] == core)
        def _():
            work(own_ref, core)
            work(other_ref, 1 - core)


def parts_kernel(start, width, which_ref, rows_ref, weight_ref, *rest):
    rows = rows_ref[:, which_ref[0], :, :width].reshape(-1, width)
    weight = weight_ref[:, :, start : start + width].reshape(-1, width)
    value = dot(rows, weight, 1, 1)
    if len(rest) == 1:
        rest[0][...] = value
        return
    got_ref, out_ref = rest
    tok, feat = out_ref.shape[2:]
    value = (value + got_ref[...]).astype(BF)
    for x in range(4):
        for y in range(4):
            out_ref[x, y] = value[x * tok : (x + 1) * tok, y * feat : (y + 1) * feat]


def grads_kernel(place_ref, pieces_ref, rows_ref, gate_ref, up_ref, down_ref):
    part = gate_ref.shape[0]
    zh, core = place_ref[0], place_ref[1]
    width = 2 * pieces_ref.shape[6]

    def side(array, y, parity):
        far = jnp.where(zh == parity, 0, 1)
        rows = []
        for x in range(4):
            for k in range(2):
                other = jnp.where(core == k, 0, 1)
                rows.append(pieces_ref[far, other, x, y, array])
        return jnp.concatenate(rows, axis=0)

    for y in range(4):
        at = slice(y * width, (y + 1) * width)
        right = jnp.concatenate([side(0, y, 0), side(0, y, 1)], axis=1)
        pair = dot(rows_ref[: 2 * part], right, 1, 0).astype(BF)
        gate_ref[:, at] = pair[:part]
        up_ref[:, at] = pair[part:]
        right = jnp.concatenate([side(1, y, 0), side(1, y, 1)], axis=1)
        down_ref[:, at] = dot(rows_ref[2 * part :], right, 1, 0).astype(BF)


def local_call(kernel, shape, scalars, *arrays):
    smem = pl.BlockSpec(memory_space=pltpu.SMEM)
    vmem = pl.BlockSpec(memory_space=pltpu.VMEM)
    return pl.pallas_call(
        kernel,
        out_shape=shape,
        in_specs=[smem] + [vmem] * len(arrays),
        out_specs=jax.tree.map(lambda _: vmem, shape),
        compiler_params=pltpu.CompilerParams(vmem_limit_bytes=40 * 2**20),
        cost_estimate=pl.CostEstimate(flops=0, bytes_accessed=0, transcendentals=0),
    )(scalars, *arrays)


def gather_plane(both):
    both = jnp.broadcast_to(both[None], (16,) + both.shape)
    own = lax.all_to_all(both, ("x", "y"), 0, 0, tiled=True)
    own = own.reshape((4, 4) + own.shape[1:])
    return own, swap(own, "c")


def per_device(tokens, cotangent, gate_weight, up_weight, down_weight):
    x, zh, core = (lax.axis_index(name) for name in ("x", "zh", "c"))
    tok, feat = tokens.shape
    cols = gate_weight.shape[1] // 4
    wide = 3 * cols

    both = jnp.stack([tokens, cotangent])

    mixed = jnp.concatenate(
        [
            gate_weight.reshape(tok, 4, cols),
            up_weight.reshape(tok, 4, cols),
            down_weight.T.reshape(tok, 4, cols),
        ],
        axis=2,
    ).transpose(1, 0, 2)
    near = lax.ppermute(both, ("zh", "c"), TURN)
    weight = jnp.zeros_like(mixed)
    weight = lax.dynamic_update_index_in_dim(weight, take(mixed, x), x, 0)
    for by in (1, 2, 3):
        sent = lax.ppermute(
            take(mixed, lax.rem(x + by, 4)), "x", [(i, (i + by) % 4) for i in range(4)]
        )
        weight = lax.dynamic_update_index_in_dim(weight, sent, lax.rem(x + 4 - by, 4), 0)

    own, other = gather_plane(near)

    part = local_call(
        partial_kernel,
        jax.ShapeDtypeStruct((4, 2, tok, wide), F32),
        jnp.stack([core]),
        own,
        other,
        weight,
    )
    both, part = lax.optimization_barrier((both, part))
    total = lax.psum_scatter(
        part.reshape(8 * tok, wide), DEPTH, scatter_dimension=0, tiled=True
    )

    far = lax.ppermute(both, ("zh", "c"), [(0, 2), (1, 0), (2, 3), (3, 1)])
    pieces = jnp.stack([own, other, *gather_plane(far)])
    pieces = pieces.reshape((2, 2) + own.shape)

    gate, upper, hidden_grad = (total[:, i * cols : (i + 1) * cols] for i in range(3))
    sigma = jax.nn.sigmoid(gate)
    activated = gate * sigma
    hidden = (activated * upper).astype(BF)
    gate_delta = (hidden_grad * upper * sigma * (1.0 + gate * (1.0 - sigma))).astype(BF)
    up_delta = (hidden_grad * activated).astype(BF)
    mine = jnp.concatenate([gate_delta, up_delta, hidden], axis=1)
    mine, hidden, pieces = lax.optimization_barrier((mine, hidden, pieces))
    every = lax.all_gather(mine, DEPTH, axis=0, tiled=True)
    hidden = gather_depth(hidden)

    def reduced(rows, start, width):
        rows = rows.reshape(4, 2, tok, rows.shape[1])
        kernel = functools.partial(parts_kernel, start, width)
        give = local_call(
            kernel,
            jax.ShapeDtypeStruct((4 * tok, 4 * feat), F32),
            jnp.stack([1 - core]),
            rows,
            weight,
        )
        sums = local_call(
            kernel,
            jax.ShapeDtypeStruct((4, 4, tok, feat), BF),
            jnp.stack([core]),
            rows,
            weight,
            swap(give, "c"),
        )
        return sums.reshape(16, tok, feat)

    def over_plane(sums):
        sums = lax.all_to_all(sums, ("x", "y"), 0, 0, tiled=True)
        return jnp.sum(sums.astype(F32), axis=0).astype(BF)

    half = cols // 2
    place = jnp.stack([zh, core])
    grad = jax.ShapeDtypeStruct((half, 8 * feat), BF)

    def own_half(rows):
        return jnp.concatenate(
            [
                jnp.where(
                    zh == 0, rows[:, at : at + half], rows[:, at + half : at + cols]
                )
                for at in range(0, rows.shape[1], cols)
            ],
            axis=1,
        ).T

    output = over_plane(reduced(hidden, 2 * cols, cols))
    every, output = lax.optimization_barrier((every, output))
    input_grad = over_plane(reduced(every, 0, 2 * cols))
    gate_grad, up_grad, down_grad = local_call(
        grads_kernel, (grad, grad, grad), place, pieces, own_half(every)
    )
    result = jnp.stack([output, input_grad])
    result, gate_grad, up_grad, down_grad = lax.optimization_barrier(
        (result, gate_grad, up_grad, down_grad)
    )
    result = lax.ppermute(result, ("zh", "c"), TURN)
    return result[0], result[1], gate_grad.T, up_grad.T, down_grad


def solution(mesh):
    fine = Mesh(mesh.devices.reshape(4, 2, 4, 2, 8), ("x", "zh", "y", "c", "gz"))
    gx, gy = ("x", "zh"), ("y", "c")
    act = P(gx, ("gz",) + gy)
    return jax.shard_map(
        per_device,
        mesh=fine,
        in_specs=(act, act, P(("gz",) + gx, gy), P(("gz",) + gx, gy), P(gy, ("gz",) + gx)),
        out_specs=(act, act, P("gz", gy + gx), P("gz", gy + gx), P(gy + gx, "gz")),
        check_vma=False,
    )
```

```python
import functools

import jax
import jax.numpy as jnp
from jax import lax
from jax.experimental import pallas as pl
from jax.experimental.pallas import tpu as pltpu
from jax.sharding import Mesh, PartitionSpec as P

BF = jnp.bfloat16
F32 = jnp.float32
DEPTH = ("zh", "gz")
TURN = [(0, 0), (1, 2), (2, 1), (3, 3)]


def dot(left, right, left_dim, right_dim):
    return lax.dot_general(
        left, right, (((left_dim,), (right_dim,)), ((), ())), preferred_element_type=F32
    )


def swap(value, axis):
    return lax.ppermute(value, axis, [(0, 1), (1, 0)])


def take(value, index, dim=0):
    return lax.dynamic_index_in_dim(value, index, dim, keepdims=False)


def tokens_of(ref, array, ys):
    return jnp.concatenate(
        [jnp.concatenate([ref[x, y, array] for x in range(4)], axis=0) for y in ys],
        axis=1,
    )


def partial_kernel(core_ref, own_ref, other_ref, weight_ref, out_ref):
    cols = weight_ref.shape[2] // 3
    tok = own_ref.shape[3]
    weight = weight_ref[...].reshape(-1, 3 * cols)

    def work(ref, k):
        pair = dot(tokens_of(ref, 0, range(4)), weight[:, : 2 * cols], 1, 0)
        last = dot(tokens_of(ref, 1, range(4)), weight[:, 2 * cols :], 1, 0)
        out_ref[:, k, :, : 2 * cols] = pair.reshape(4, tok, 2 * cols)
        out_ref[:, k, :, 2 * cols :] = last.reshape(4, tok, cols)

    for core in range(2):

        @pl.when(core_ref[0] == core)
        def _():
            work(own_ref, core)
            work(other_ref, 1 - core)


def parts_kernel(start, rows_ref, weight_ref, out_ref):
    tok, feat = out_ref.shape[3:]
    width = rows_ref.shape[3]
    weight = weight_ref[:, :, start : start + width].reshape(-1, width)
    for x in range(4):
        value = dot(rows_ref[x].reshape(2 * tok, width), weight, 1, 1).astype(BF)
        for y in range(4):
            for k in range(2):
                out_ref[x, y, k] = value[
                    k * tok : (k + 1) * tok, y * feat : (y + 1) * feat
                ]


def grads_kernel(
    place_ref, pieces_ref, deltas_ref, hidden_ref, gate_ref, up_ref, down_ref
):
    part = gate_ref.shape[0]
    zh, core = place_ref[0], place_ref[1]
    width = 2 * pieces_ref.shape[6]

    def side(array, y, parity):
        far = jnp.where(zh == parity, 0, 1)
        rows = []
        for x in range(4):
            for k in range(2):
                other = jnp.where(core == k, 0, 1)
                rows.append(pieces_ref[far, other, x, y, array])
        return jnp.concatenate(rows, axis=0)

    for y in range(4):
        at = slice(y * width, (y + 1) * width)
        right = jnp.concatenate([side(0, y, 0), side(0, y, 1)], axis=1)
        pair = dot(deltas_ref[...], right, 1, 0).astype(BF)
        gate_ref[:, at] = pair[:part]
        up_ref[:, at] = pair[part:]
        right = jnp.concatenate([side(1, y, 0), side(1, y, 1)], axis=1)
        down_ref[:, at] = dot(hidden_ref[...], right, 1, 0).astype(BF)


def local_call(kernel, shape, arrays, *scalars):
    smem = pl.BlockSpec(memory_space=pltpu.SMEM)
    vmem = pl.BlockSpec(memory_space=pltpu.VMEM)
    return pl.pallas_call(
        kernel,
        out_shape=shape,
        in_specs=[smem] * len(scalars) + [vmem] * len(arrays),
        out_specs=jax.tree.map(lambda _: vmem, shape),
        compiler_params=pltpu.CompilerParams(vmem_limit_bytes=40 * 2**20),
        cost_estimate=pl.CostEstimate(flops=0, bytes_accessed=0, transcendentals=0),
    )(*scalars, *arrays)


def gather_plane(both):
    both = jnp.broadcast_to(both[None], (16,) + both.shape)
    own = lax.all_to_all(both, ("x", "y"), 0, 0, tiled=True)
    own = own.reshape((4, 4) + own.shape[1:])
    return own, swap(own, "c")


def per_device(tokens, cotangent, gate_weight, up_weight, down_weight):
    x, zh, core = (lax.axis_index(name) for name in ("x", "zh", "c"))
    tok, feat = tokens.shape
    cols = gate_weight.shape[1] // 4
    wide = 3 * cols

    both = jnp.stack([tokens, cotangent])

    mixed = jnp.concatenate(
        [
            gate_weight.reshape(tok, 4, cols),
            up_weight.reshape(tok, 4, cols),
            down_weight.T.reshape(tok, 4, cols),
        ],
        axis=2,
    ).transpose(1, 0, 2)
    near = lax.ppermute(both, ("zh", "c"), TURN)
    weight = jnp.zeros_like(mixed)
    weight = lax.dynamic_update_index_in_dim(weight, take(mixed, x), x, 0)
    for by in (1, 2, 3):
        sent = lax.ppermute(
            take(mixed, lax.rem(x + by, 4)), "x", [(i, (i + by) % 4) for i in range(4)]
        )
        weight = lax.dynamic_update_index_in_dim(weight, sent, lax.rem(x + 4 - by, 4), 0)

    own, other = gather_plane(near)

    part = local_call(
        partial_kernel,
        jax.ShapeDtypeStruct((4, 2, tok, wide), F32),
        (own, other, weight),
        jnp.stack([core]),
    )
    both, part = lax.optimization_barrier((both, part))
    total = lax.psum_scatter(
        part.reshape(8 * tok, wide), DEPTH, scatter_dimension=0, tiled=True
    )

    far = lax.ppermute(both, ("zh", "c"), [(0, 2), (1, 0), (2, 3), (3, 1)])
    pieces = jnp.stack([own, other, *gather_plane(far)])
    pieces = pieces.reshape((2, 2) + own.shape)

    gate, upper, hidden_grad = (total[:, i * cols : (i + 1) * cols] for i in range(3))
    sigma = jax.nn.sigmoid(gate)
    activated = gate * sigma
    hidden = (activated * upper).astype(BF)
    gate_delta = (hidden_grad * upper * sigma * (1.0 + gate * (1.0 - sigma))).astype(BF)
    up_delta = (hidden_grad * activated).astype(BF)
    mine = jnp.concatenate([gate_delta, up_delta], axis=1)
    mine, hidden, pieces = lax.optimization_barrier((mine, hidden, pieces))
    deltas = lax.all_gather(mine, DEPTH, axis=0, tiled=True)
    hidden = lax.all_gather(hidden, DEPTH, axis=0, tiled=True)

    def reduced(rows, start):
        sums = local_call(
            functools.partial(parts_kernel, start),
            jax.ShapeDtypeStruct((4, 4, 2, tok, feat), BF),
            (rows.reshape(4, 2, tok, rows.shape[1]), weight),
        )
        sums = sums.reshape(32, tok, feat)
        sums = lax.all_to_all(sums, ("x", "y", "c"), 0, 0, tiled=True)
        return jnp.sum(sums.astype(F32), axis=0).astype(BF)

    half = cols // 2
    place = jnp.stack([zh, core])
    grad = jax.ShapeDtypeStruct((half, 8 * feat), BF)

    def own_half(rows):
        return jnp.concatenate(
            [
                jnp.where(
                    zh == 0, rows[:, at : at + half], rows[:, at + half : at + cols]
                )
                for at in range(0, rows.shape[1], cols)
            ],
            axis=1,
        ).T

    output = reduced(hidden, 2 * cols)
    deltas, output = lax.optimization_barrier((deltas, output))
    input_grad = reduced(deltas, 0)
    gate_grad, up_grad, down_grad = local_call(
        grads_kernel,
        (grad, grad, grad),
        (pieces, own_half(deltas), own_half(hidden)),
        place,
    )
    result = jnp.stack([output, input_grad])
    result, gate_grad, up_grad, down_grad = lax.optimization_barrier(
        (result, gate_grad, up_grad, down_grad)
    )
    result = lax.ppermute(result, ("zh", "c"), TURN)
    return result[0], result[1], gate_grad.T, up_grad.T, down_grad


def solution(mesh):
    fine = Mesh(mesh.devices.reshape(4, 2, 4, 2, 8), ("x", "zh", "y", "c", "gz"))
    gx, gy = ("x", "zh"), ("y", "c")
    act = P(gx, ("gz",) + gy)
    return jax.shard_map(
        per_device,
        mesh=fine,
        in_specs=(act, act, P(("gz",) + gx, gy), P(("gz",) + gx, gy), P(gy, ("gz",) + gx)),
        out_specs=(act, act, P("gz", gy + gx), P("gz", gy + gx), P(gy + gx, "gz")),
        check_vma=False,
    )
```

```python
import functools

import jax
import jax.numpy as jnp
from jax import lax
from jax.experimental import pallas as pl
from jax.experimental.pallas import tpu as pltpu
from jax.sharding import Mesh, PartitionSpec as P

BF = jnp.bfloat16
F32 = jnp.float32
DEPTH = ("zh", "gz")
TURN = [(0, 0), (1, 2), (2, 1), (3, 3)]


def dot(left, right, left_dim, right_dim):
    return lax.dot_general(
        left, right, (((left_dim,), (right_dim,)), ((), ())), preferred_element_type=F32
    )


def swap(value, axis):
    return lax.ppermute(value, axis, [(0, 1), (1, 0)])


def take(value, index, dim=0):
    return lax.dynamic_index_in_dim(value, index, dim, keepdims=False)


def tokens_of(ref, array, ys):
    return jnp.concatenate(
        [jnp.concatenate([ref[x, y, array] for x in range(4)], axis=0) for y in ys],
        axis=1,
    )


def partial_kernel(core_ref, own_ref, other_ref, weight_ref, out_ref):
    cols = weight_ref.shape[2] // 3
    tok = own_ref.shape[3]
    weight = weight_ref[...].reshape(-1, 3 * cols)

    def work(ref, k):
        pair = dot(tokens_of(ref, 0, range(4)), weight[:, : 2 * cols], 1, 0)
        last = dot(tokens_of(ref, 1, range(4)), weight[:, 2 * cols :], 1, 0)
        out_ref[:, k, :, : 2 * cols] = pair.reshape(4, tok, 2 * cols)
        out_ref[:, k, :, 2 * cols :] = last.reshape(4, tok, cols)

    for core in range(2):

        @pl.when(core_ref[0] == core)
        def _():
            work(own_ref, core)
            work(other_ref, 1 - core)


def parts_kernel(start, rows_ref, weight_ref, out_ref):
    tok, feat = out_ref.shape[3:]
    width = rows_ref.shape[3]
    weight = weight_ref[:, :, start : start + width].reshape(-1, width)
    for x in range(4):
        value = dot(rows_ref[x].reshape(2 * tok, width), weight, 1, 1).astype(BF)
        for y in range(4):
            for k in range(2):
                out_ref[x, y, k] = value[
                    k * tok : (k + 1) * tok, y * feat : (y + 1) * feat
                ]


def grads_kernel(
    place_ref, pieces_ref, deltas_ref, hidden_ref, gate_ref, up_ref, down_ref
):
    part = gate_ref.shape[0]
    zh, core = place_ref[0], place_ref[1]
    width = 2 * pieces_ref.shape[6]

    def side(array, y, parity):
        far = jnp.where(zh == parity, 0, 1)
        rows = []
        for x in range(4):
            for k in range(2):
                other = jnp.where(core == k, 0, 1)
                rows.append(pieces_ref[far, other, x, y, array])
        return jnp.concatenate(rows, axis=0)

    for y in range(4):
        at = slice(y * width, (y + 1) * width)
        right = jnp.concatenate([side(0, y, 0), side(0, y, 1)], axis=1)
        pair = dot(deltas_ref[...], right, 1, 0).astype(BF)
        gate_ref[:, at] = pair[:part]
        up_ref[:, at] = pair[part:]
        right = jnp.concatenate([side(1, y, 0), side(1, y, 1)], axis=1)
        down_ref[:, at] = dot(hidden_ref[...], right, 1, 0).astype(BF)


def local_call(kernel, shape, arrays, *scalars):
    smem = pl.BlockSpec(memory_space=pltpu.SMEM)
    vmem = pl.BlockSpec(memory_space=pltpu.VMEM)
    return pl.pallas_call(
        kernel,
        out_shape=shape,
        in_specs=[smem] * len(scalars) + [vmem] * len(arrays),
        out_specs=jax.tree.map(lambda _: vmem, shape),
        compiler_params=pltpu.CompilerParams(vmem_limit_bytes=40 * 2**20),
        cost_estimate=pl.CostEstimate(flops=0, bytes_accessed=0, transcendentals=0),
    )(*scalars, *arrays)


def gather_plane(both):
    both = jnp.broadcast_to(both[None], (16,) + both.shape)
    own = lax.all_to_all(both, ("x", "y"), 0, 0, tiled=True)
    own = own.reshape((4, 4) + own.shape[1:])
    return own, swap(own, "c")


def per_device(tokens, cotangent, gate_weight, up_weight, down_weight):
    x, zh, core = (lax.axis_index(name) for name in ("x", "zh", "c"))
    tok, feat = tokens.shape
    cols = gate_weight.shape[1] // 4
    wide = 3 * cols

    both = jnp.stack([tokens, cotangent])

    mixed = jnp.concatenate(
        [
            gate_weight.reshape(tok, 4, cols),
            up_weight.reshape(tok, 4, cols),
            down_weight.T.reshape(tok, 4, cols),
        ],
        axis=2,
    ).transpose(1, 0, 2)
    near = lax.ppermute(both, ("zh", "c"), TURN)
    weight = jnp.zeros_like(mixed)
    weight = lax.dynamic_update_index_in_dim(weight, take(mixed, x), x, 0)
    for by in (1, 2, 3):
        sent = lax.ppermute(
            take(mixed, lax.rem(x + by, 4)), "x", [(i, (i + by) % 4) for i in range(4)]
        )
        weight = lax.dynamic_update_index_in_dim(weight, sent, lax.rem(x + 4 - by, 4), 0)

    own, other = gather_plane(near)

    part = local_call(
        partial_kernel,
        jax.ShapeDtypeStruct((4, 2, tok, wide), F32),
        (own, other, weight),
        jnp.stack([core]),
    )
    both, part = lax.optimization_barrier((both, part))
    total = lax.psum_scatter(
        part.reshape(8 * tok, wide), DEPTH, scatter_dimension=0, tiled=True
    )

    far = lax.ppermute(both, ("zh", "c"), [(0, 2), (1, 0), (2, 3), (3, 1)])
    pieces = jnp.stack([own, other, *gather_plane(far)])
    pieces = pieces.reshape((2, 2) + own.shape)

    gate, upper, hidden_grad = (total[:, i * cols : (i + 1) * cols] for i in range(3))
    sigma = jax.nn.sigmoid(gate)
    activated = gate * sigma
    hidden = (activated * upper).astype(BF)
    gate_delta = (hidden_grad * upper * sigma * (1.0 + gate * (1.0 - sigma))).astype(BF)
    up_delta = (hidden_grad * activated).astype(BF)
    mine = jnp.concatenate([gate_delta, up_delta], axis=1)
    mine, hidden, pieces = lax.optimization_barrier((mine, hidden, pieces))
    deltas = lax.all_gather(mine, DEPTH, axis=0, tiled=True)
    hidden = lax.all_gather(hidden, DEPTH, axis=0, tiled=True)

    def reduced(rows, start):
        sums = local_call(
            functools.partial(parts_kernel, start),
            jax.ShapeDtypeStruct((4, 4, 2, tok, feat), BF),
            (rows.reshape(4, 2, tok, rows.shape[1]), weight),
        )
        sums = sums.reshape(32, tok, feat)
        sums = lax.all_to_all(sums, ("x", "y", "c"), 0, 0, tiled=True)
        return jnp.sum(sums.astype(F32), axis=0).astype(BF)

    half = cols // 2
    place = jnp.stack([zh, core])
    grad = jax.ShapeDtypeStruct((half, 8 * feat), BF)

    def own_half(rows):
        return jnp.concatenate(
            [
                jnp.where(
                    zh == 0, rows[:, at : at + half], rows[:, at + half : at + cols]
                )
                for at in range(0, rows.shape[1], cols)
            ],
            axis=1,
        ).T

    output = reduced(hidden, 2 * cols)
    hidden = own_half(hidden)
    deltas, output, hidden = lax.optimization_barrier((deltas, output, hidden))
    output = lax.ppermute(output, ("zh", "c"), TURN)
    input_grad = reduced(deltas, 0)
    grads = local_call(
        grads_kernel,
        (grad, grad, grad),
        (pieces, own_half(deltas), hidden),
        place,
    )
    input_grad, grads = lax.optimization_barrier((input_grad, grads))
    gate_grad, up_grad, down_grad = grads
    input_grad = lax.ppermute(input_grad, ("zh", "c"), TURN)
    return output, input_grad, gate_grad.T, up_grad.T, down_grad


def solution(mesh):
    fine = Mesh(mesh.devices.reshape(4, 2, 4, 2, 8), ("x", "zh", "y", "c", "gz"))
    gx, gy = ("x", "zh"), ("y", "c")
    act = P(gx, ("gz",) + gy)
    return jax.shard_map(
        per_device,
        mesh=fine,
        in_specs=(act, act, P(("gz",) + gx, gy), P(("gz",) + gx, gy), P(gy, ("gz",) + gx)),
        out_specs=(act, act, P("gz", gy + gx), P("gz", gy + gx), P(gy + gx, "gz")),
        check_vma=False,
    )
```
